512 devices in a mesh: row: 16 (over y_hi, x), col: 32 (over y_lo, z, core).
Axes of the slice: x: 4, y: 8 (y_hi: 4, y_lo: 2; y = y_hi * 2 + y_lo), z: 8, core: 2. Of those that a mesh axis runs over, the one named last changes fastest.
Arguments:
- inputs: bfloat16 [1024, 16384], P('col', 'row'), may hold values from -0.1875 to 0.1875
- weight: bfloat16 [16384, 18432], P('row', 'col'), may hold values from -0.046875 to 0.046875
- grad_out: bfloat16 [1024, 18432], P('row', 'col'), may hold values from -6 to 6
- positions: int32 [1024], P('row'), may hold values from 0 to 8191
Outputs:
- input_grad: bfloat16 [1024, 16384], P('col', 'row')
- weight_grad: float32 [16384, 18432], P('row', 'col')
The draws below stay inside these ranges and needn't reach their ends.
All inputs are finite; a program needn't handle non-finite values.
Results may differ from the reference program's by a relative error of at most 0.0065.
Values may be sent and summed in bfloat16 or wider, within the bound.
No kernel may reach another device: no remote copies, remote signals or barrier semaphores. Data moves between devices by JAX's collectives and lax.ppermute only.
A program may use at most 64 MiB of HBM per device.

```python
import math
import jax
import jax.numpy as jnp
from jax import lax

D = 16384
QHEADS = 128
KVHEADS = 8
HEAD = 128
F = 18432
TOKENS = 1024


def set_ends(result, own_key, least, largest):
    dims = result.shape
    place = [jax.random.randint(jax.random.fold_in(own_key, axis), (), 0, dims[axis]) for axis in range(len(dims))]
    result = result.at[tuple(place)].set(least)
    longest = dims.index(max(dims))
    place[longest] = (place[longest] + 1) % dims[longest]
    return result.at[tuple(place)].set(largest)


def block_levels(rng, shape, cuts, least, high):
    gain, own = 1.0, jax.random.fold_in(rng, 6)
    for position, parts in cuts:
        heights = jnp.exp(jax.random.uniform(jax.random.fold_in(own, position), (parts,), jnp.float32, least / len(cuts), high / len(cuts)))
        gain = gain * jnp.repeat(heights, shape[position] // parts).reshape([-1 if axis == position else 1 for axis in range(len(shape))])
    return gain


def centred(key, shape, deviation, bound, shards=(), held_as=jnp.bfloat16):
    loudness = block_levels(key, shape, shards, -0.22, 0.18) if shards else 1.0
    values = jax.random.normal(key, shape, jnp.float32) * deviation * loudness
    return jnp.minimum(jnp.maximum(values, -bound), bound).astype(held_as)


def setup_inputs(seed: int = 0) -> dict:
    key_list = jax.random.split(jax.random.key(seed), 5)
    inputs = centred(key_list[0], (TOKENS, D), (TOKENS ** -0.5), 0.1875, ((0, 32), (1, 16)))
    weight = centred(key_list[1], (D, F), D ** -0.5, 0.046875, ((0, 16), (1, 32)))
    grad_out = centred(key_list[2], (TOKENS, F), 1.0, 6.0, ((0, 16), (1, 32)))
    positions = set_ends(jax.random.randint(key_list[3], (TOKENS,), 0, 8192), jax.random.fold_in(key_list[3], 1), 0, 8191).astype(jnp.int32)
    return {"inputs": inputs, "weight": weight, "grad_out": grad_out, "positions": positions}


def scaled_freq(within):
    base = jnp.exp(-(2.0 * within.astype(jnp.float32) / HEAD) * math.log(500000.0))
    wave = 2.0 * math.pi / base
    smooth = (8192.0 / wave - 1.0) / 3.0
    middle = (1.0 - smooth) * base / 8.0 + smooth * base
    return jnp.where(wave < 2048.0, base, jnp.where(wave > 8192.0, base / 8.0, middle))


def unrotate(grad, positions, col_start):
    rows = grad.shape[0]
    pairs = grad.shape[1] // 2
    columns = col_start + 2 * jnp.arange(pairs, dtype=jnp.int32)
    within = (columns % HEAD) // 2
    freq = scaled_freq(within)
    angle = positions.astype(jnp.float32)[:, None] * freq[None, :]
    cosine = jnp.cos(angle)
    sine = jnp.sin(angle)
    rotated = (columns < (QHEADS + KVHEADS) * HEAD)[None, :]
    cosine = jnp.where(rotated, cosine, 1.0)
    sine = jnp.where(rotated, sine, 0.0)
    split = grad.astype(jnp.float32).reshape(rows, pairs, 2)
    first = split[:, :, 0]
    second = split[:, :, 1]
    new_first = first * cosine + second * sine
    new_second = second * cosine - first * sine
    return jnp.stack([new_first, new_second], axis=2).reshape(rows, 2 * pairs).astype(jnp.bfloat16)


def reference(inputs, weight, grad_out, positions):
    grad = unrotate(grad_out, positions, 0)
    input_grad = lax.dot_general(grad, weight, (((1,), (1,)), ((), ())), preferred_element_type=jnp.float32).astype(jnp.bfloat16)
    weight_grad = lax.dot_general(inputs, grad, (((0,), (0,)), ((), ())), preferred_element_type=jnp.float32)
    return input_grad, weight_grad
```

```python
import math

import jax
import jax.numpy as jnp
from jax import lax
from jax.experimental import pallas as pl
from jax.experimental.pallas import tpu as pltpu
from jax.sharding import Mesh, PartitionSpec as P

QHEADS = 128
KVHEADS = 8
HEAD = 128
ROTATED = (QHEADS + KVHEADS) * HEAD

HALF_PI = (1.5703125, 4.837512969970703e-4, 7.549789948768648e-8)
ROW = ("yh", "x")
COL = ("yl", "zh", "zl", "c")
OWNERS = ("zl", "yl", "zh")
SWAP = ((0, 1), (1, 0))


def scaled_freq(within):
    base = jnp.exp(-(2.0 * within.astype(jnp.float32) / HEAD) * math.log(500000.0))
    wave = 2.0 * math.pi / base
    smooth = (8192.0 / wave - 1.0) / 3.0
    middle = (1.0 - smooth) * base / 8.0 + smooth * base
    return jnp.where(wave < 2048.0, base, jnp.where(wave > 8192.0, base / 8.0, middle))


def sine_cosine(angle):
    turns = jnp.floor(angle * (2.0 / math.pi) + 0.5)
    rest = angle
    for part in HALF_PI:
        rest = rest - turns * part
    square = rest * rest
    sine = rest + rest * square * (
        -1.6666654611e-1 + square * (8.3321608736e-3 + square * -1.9515295891e-4)
    )
    cosine = (
        1.0
        - 0.5 * square
        + square * square * (4.166664568298827e-2 + square * (-1.388731625493765e-3 + square * 2.443315711809948e-5))
    )
    quarter = turns.astype(jnp.int32)
    odd = (quarter & 1) == 1
    sine, cosine = jnp.where(odd, cosine, sine), jnp.where(odd, sine, cosine)
    sine = jnp.where((quarter & 2) == 2, -sine, sine)
    cosine = jnp.where(((quarter + 1) & 2) == 2, -cosine, cosine)
    return sine, cosine


def unrotate_kernel(place_ref, positions_ref, grad_ref, out_ref):
    rows, width = grad_ref.shape
    col_start, core = place_ref[0], place_ref[1]
    row = lax.broadcasted_iota(jnp.int32, (rows, rows), 0)
    column = lax.broadcasted_iota(jnp.int32, (rows, rows), 1)
    spread = jnp.where(row == column, positions_ref[...].astype(jnp.float32), 0.0)
    positions = jnp.sum(spread, axis=1, keepdims=True)
    lane = lax.broadcasted_iota(jnp.int32, (8, HEAD), 1)
    freq = scaled_freq(((col_start + lane) & (HEAD - 1)) >> 1)[:1]
    sine, cosine = sine_cosine(positions * freq)
    source = lax.broadcasted_iota(jnp.int32, (HEAD, HEAD), 0)
    target = lax.broadcasted_iota(jnp.int32, (HEAD, HEAD), 1)
    partner = jnp.where(source == (target ^ 1), jnp.where((target & 1) == 0, 1.0, -1.0), 0.0).astype(jnp.bfloat16)
    for start in range(0, width, HEAD):
        size = min(HEAD, width - start)
        block = grad_ref[:, start : start + size]
        swapped = jnp.dot(block, partner[:size, :size], preferred_element_type=jnp.float32)
        turned = block.astype(jnp.float32) * cosine[:, :size] + swapped * sine[:, :size]
        columns = col_start + start + lax.broadcasted_iota(jnp.int32, (rows, size), 1)
        result = jnp.where(columns < ROTATED, turned, block.astype(jnp.float32)).astype(jnp.bfloat16)
        half = rows // 2
        upper, lower = result[:half], result[half:]
        own = jnp.where(core == 0, upper, lower)
        other = jnp.where(core == 0, lower, upper)
        for copy in range(out_ref.shape[0]):
            out_ref[copy, :half, start : start + size] = own
            out_ref[copy, half:, start : start + size] = other


def unrotate(grad, positions, place, copies):
    rows, width = grad.shape
    return pl.pallas_call(
        unrotate_kernel,
        out_shape=jax.ShapeDtypeStruct((copies, rows, width), jnp.bfloat16),
        in_specs=[
            pl.BlockSpec(memory_space=pltpu.SMEM),
            pl.BlockSpec(memory_space=pltpu.VMEM),
            pl.BlockSpec(memory_space=pltpu.VMEM),
        ],
        out_specs=pl.BlockSpec(memory_space=pltpu.VMEM),
        name="unrotate",
    )(place, positions.reshape(1, rows), grad)


def exchange(parts, axes):
    return lax.all_to_all(parts, axes, 0, 0, tiled=True)


def copies_of(array, count):
    return jnp.broadcast_to(array[None], (count, *array.shape))


def over_width(left, right):
    return lax.dot_general(left, right, (((1,), (1,)), ((), ())), preferred_element_type=jnp.float32)


def over_tokens(left, right):
    return lax.dot_general(left, right, (((0,), (0,)), ((), ())), preferred_element_type=jnp.float32)


def per_device(inputs, weight, grad_out, positions):
    width = weight.shape[1]
    tokens, model = inputs.shape
    owners = lax.axis_size(OWNERS)
    place = jnp.stack([lax.axis_index(COL) * width, lax.axis_index("c")]).astype(jnp.int32)

    own_inputs = exchange(copies_of(inputs, owners), OWNERS).reshape(-1, model)
    other_inputs = lax.ppermute(own_inputs, "c", SWAP)

    sent = unrotate(grad_out, positions, place, lax.axis_size("yh"))
    grads = exchange(sent, "yh")
    half = grads.shape[1] // 2
    other_grads = exchange(copies_of(grads[:, half:].reshape(-1, width), lax.axis_size("x")), "x").reshape(-1, width)
    own_grads = exchange(copies_of(grads[:, :half].reshape(-1, width), lax.axis_size("x")), "x").reshape(-1, width)

    other_part = over_width(other_grads, weight).astype(jnp.bfloat16)
    arrived = lax.ppermute(other_part, "c", SWAP)
    own_part = (over_width(own_grads, weight) + arrived.astype(jnp.float32)).astype(jnp.bfloat16)
    parts = exchange(own_part.reshape(owners, tokens, model), OWNERS)
    input_grad = parts.astype(jnp.float32).sum(axis=0).astype(jnp.bfloat16)

    weight_grad = over_tokens(own_inputs, own_grads) + over_tokens(other_inputs, other_grads)
    return input_grad, weight_grad


def solution(mesh):
    sizes = {"yh": 4, "x": 4, "yl": 2, "zh": 2, "zl": 4, "c": 2}
    finer = Mesh(mesh.devices.reshape(tuple(sizes.values())), tuple(sizes))
    in_specs = (P(COL, ROW), P(ROW, COL), P(ROW, COL), P(ROW))
    out_specs = (P(COL, ROW), P(ROW, COL))
    return jax.shard_map(per_device, mesh=finer, in_specs=in_specs, out_specs=out_specs, check_vma=False)
```

```python
import math

import jax
import jax.numpy as jnp
from jax import lax
from jax.experimental import pallas as pl
from jax.experimental.pallas import tpu as pltpu
from jax.sharding import Mesh, PartitionSpec as P

QHEADS = 128
KVHEADS = 8
HEAD = 128
ROTATED = (QHEADS + KVHEADS) * HEAD

HALF_PI = (1.5703125, 4.837512969970703e-4, 7.549789948768648e-8)
ROW = ("yh", "x")
COL = ("yl", "z4", "z2", "z1", "c")
SWAP = ((0, 1), (1, 0))


def scaled_freq(within):
    base = jnp.exp(-(2.0 * within.astype(jnp.float32) / HEAD) * math.log(500000.0))
    wave = 2.0 * math.pi / base
    smooth = (8192.0 / wave - 1.0) / 3.0
    middle = (1.0 - smooth) * base / 8.0 + smooth * base
    return jnp.where(wave < 2048.0, base, jnp.where(wave > 8192.0, base / 8.0, middle))


def sine_cosine(angle):
    turns = jnp.floor(angle * (2.0 / math.pi) + 0.5)
    rest = angle
    for part in HALF_PI:
        rest = rest - turns * part
    square = rest * rest
    sine = rest + rest * square * (
        -1.6666654611e-1 + square * (8.3321608736e-3 + square * -1.9515295891e-4)
    )
    cosine = (
        1.0
        - 0.5 * square
        + square * square * (4.166664568298827e-2 + square * (-1.388731625493765e-3 + square * 2.443315711809948e-5))
    )
    quarter = turns.astype(jnp.int32)
    odd = (quarter & 1) == 1
    sine, cosine = jnp.where(odd, cosine, sine), jnp.where(odd, sine, cosine)
    sine = jnp.where((quarter & 2) == 2, -sine, sine)
    cosine = jnp.where(((quarter + 1) & 2) == 2, -cosine, cosine)
    return sine, cosine


def unrotate_kernel(place_ref, positions_ref, own_ref, other_ref, out_ref):
    rows, width = own_ref.shape
    core = place_ref[1]
    wanted = lax.broadcasted_iota(jnp.int32, (rows, 2 * rows), 0) + core * rows
    column = lax.broadcasted_iota(jnp.int32, (rows, 2 * rows), 1)
    spread = jnp.where(wanted == column, positions_ref[...].astype(jnp.float32), 0.0)
    positions = jnp.sum(spread, axis=1, keepdims=True)
    lane = lax.broadcasted_iota(jnp.int32, (8, HEAD), 1)
    source = lax.broadcasted_iota(jnp.int32, (HEAD, HEAD), 0)
    target = lax.broadcasted_iota(jnp.int32, (HEAD, HEAD), 1)
    partner = jnp.where(source == (target ^ 1), jnp.where((target & 1) == 0, 1.0, -1.0), 0.0).astype(jnp.bfloat16)
    for side, (grad_ref, col_start) in enumerate(((own_ref, place_ref[0]), (other_ref, place_ref[2]))):
        freq = scaled_freq(((col_start + lane) & (HEAD - 1)) >> 1)[:1]
        sine, cosine = sine_cosine(positions * freq)
        for start in range(0, width, HEAD):
            size = min(HEAD, width - start)
            block = grad_ref[:, start : start + size]
            swapped = jnp.dot(block, partner[:size, :size], preferred_element_type=jnp.float32)
            turned = block.astype(jnp.float32) * cosine[:, :size] + swapped * sine[:, :size]
            columns = col_start + start + lax.broadcasted_iota(jnp.int32, (rows, size), 1)
            result = jnp.where(columns < ROTATED, turned, block.astype(jnp.float32)).astype(jnp.bfloat16)
            for copy in range(out_ref.shape[0]):
                out_ref[copy, :, side * width + start : side * width + start + size] = result


def unrotate(own, other, positions, place, copies):
    rows, width = own.shape
    return pl.pallas_call(
        unrotate_kernel,
        out_shape=jax.ShapeDtypeStruct((copies, rows, 2 * width), jnp.bfloat16),
        in_specs=[pl.BlockSpec(memory_space=pltpu.SMEM)] + [pl.BlockSpec(memory_space=pltpu.VMEM)] * 3,
        out_specs=pl.BlockSpec(memory_space=pltpu.VMEM),
        name="unrotate",
    )(place, positions.reshape(1, 2 * rows), own, other)


def exchange(parts, axes):
    return lax.all_to_all(parts, axes, 0, 0, tiled=True)


def copies_of(array, count):
    return jnp.broadcast_to(array[None], (count, *array.shape))


def swapped(array, axis):
    return lax.ppermute(array, axis, SWAP)


def in_order(own, other, axis, dim):
    first = lax.axis_index(axis) == 0
    return jnp.concatenate([jnp.where(first, own, other), jnp.where(first, other, own)], dim)


def contract(left, right, left_dim, right_dim):
    dims = (((left_dim,), (right_dim,)), ((), ()))
    return lax.dot_general(left, right, dims, preferred_element_type=jnp.float32)


def per_device(inputs, weight, grad_out, positions):
    width = weight.shape[1]
    tokens, model = inputs.shape
    core = lax.axis_index("c")
    col_start = lax.axis_index(COL) * width
    place = jnp.stack([col_start, core, col_start + (1 - 2 * core) * width]).astype(jnp.int32)

    upper, lower = grad_out[:tokens], grad_out[tokens:]
    first = core == 0
    other_raw = swapped(jnp.where(first, lower, upper), "c")
    sent = unrotate(jnp.where(first, upper, lower), other_raw, positions, place, lax.axis_size("yh"))
    sent, inputs, weight = lax.optimization_barrier((sent, inputs, weight))
    other_weight = swapped(weight, "c")

    own_inputs = inputs.reshape(1, 1, 1, tokens, model)
    for dim, axis in ((2, "z4"), (0, "z2"), (1, "z1")):
        own_inputs = in_order(own_inputs, swapped(own_inputs, axis), axis, dim)
    own_inputs = own_inputs.reshape(4, 2 * tokens, model)
    own_inputs = jnp.stack([own_inputs, swapped(own_inputs, "yl")], 1).reshape(-1, model)
    other_inputs = swapped(own_inputs, "c")

    grads = exchange(sent, "yh").reshape(2, -1, 2 * width)
    yl = lax.axis_index("yl") == 0
    grads = jnp.stack([jnp.where(yl, grads[0], grads[1]), jnp.where(yl, grads[1], grads[0])])
    grads = exchange(copies_of(grads, lax.axis_size("x")), "x")
    own_columns = grads[..., :width].reshape(-1, width)
    other_columns = swapped(grads[..., width:].reshape(-1, width), "c")

    both = jnp.concatenate([weight, other_weight], 1)
    far = contract(grads[:, 1].reshape(-1, 2 * width), both, 1, 1).astype(jnp.bfloat16)
    arrived = swapped(far, "yl").astype(jnp.float32)
    near = (contract(grads[:, 0].reshape(-1, 2 * width), both, 1, 1) + arrived).astype(jnp.bfloat16)
    parts = exchange(near.reshape(8, tokens, model), ("z2", "z1", "z4"))
    input_grad = parts.astype(jnp.float32).sum(axis=0).astype(jnp.bfloat16)

    weight_grad = contract(own_inputs, own_columns, 0, 0) + contract(other_inputs, other_columns, 0, 0)
    return input_grad, weight_grad


def solution(mesh):
    sizes = {"yh": 4, "x": 4, "yl": 2, "z4": 2, "z2": 2, "z1": 2, "c": 2}
    finer = Mesh(mesh.devices.reshape(tuple(sizes.values())), tuple(sizes))
    in_specs = (P(COL, ROW), P(ROW, COL), P(ROW, COL), P(ROW))
    out_specs = (P(COL, ROW), P(ROW, COL))
    return jax.shard_map(per_device, mesh=finer, in_specs=in_specs, out_specs=out_specs, check_vma=False)
```

```python
import math

import jax
import jax.numpy as jnp
from jax import lax
from jax.experimental import pallas as pl
from jax.experimental.pallas import tpu as pltpu
from jax.sharding import Mesh, PartitionSpec as P

QHEADS = 128
KVHEADS = 8
HEAD = 128
ROTATED = (QHEADS + KVHEADS) * HEAD

HALF_PI = (1.5703125, 4.837512969970703e-4, 7.549789948768648e-8)
ROW = ("yh", "x")
COL = ("yl", "z4", "z2", "z1", "c")
SWAP = ((0, 1), (1, 0))
STEP = 256


def scaled_freq(within):
    base = jnp.exp(-(2.0 * within.astype(jnp.float32) / HEAD) * math.log(500000.0))
    wave = 2.0 * math.pi / base
    smooth = (8192.0 / wave - 1.0) / 3.0
    middle = (1.0 - smooth) * base / 8.0 + smooth * base
    return jnp.where(wave < 2048.0, base, jnp.where(wave > 8192.0, base / 8.0, middle))


def sine_cosine(angle):
    turns = jnp.floor(angle * (2.0 / math.pi) + 0.5)
    rest = angle
    for part in HALF_PI:
        rest = rest - turns * part
    square = rest * rest
    sine = rest + rest * square * (
        -1.6666654611e-1 + square * (8.3321608736e-3 + square * -1.9515295891e-4)
    )
    cosine = (
        1.0
        - 0.5 * square
        + square * square * (4.166664568298827e-2 + square * (-1.388731625493765e-3 + square * 2.443315711809948e-5))
    )
    quarter = turns.astype(jnp.int32)
    odd = (quarter & 1) == 1
    sine, cosine = jnp.where(odd, cosine, sine), jnp.where(odd, sine, cosine)
    sine = jnp.where((quarter & 2) == 2, -sine, sine)
    cosine = jnp.where(((quarter + 1) & 2) == 2, -cosine, cosine)
    return sine, cosine


def unrotate_kernel(positions_ref, grad_ref, out_ref):
    rows, width = grad_ref.shape
    col_start = lax.axis_index(COL) * width
    row = lax.broadcasted_iota(jnp.int32, (rows, rows), 0)
    column = lax.broadcasted_iota(jnp.int32, (rows, rows), 1)
    spread = jnp.where(row == column, positions_ref[...].astype(jnp.float32), 0.0)
    positions = jnp.sum(spread, axis=1, keepdims=True)
    lane = lax.broadcasted_iota(jnp.int32, (8, HEAD), 1)
    freq = scaled_freq(((col_start + lane) & (HEAD - 1)) >> 1)[:1]
    sine, cosine = sine_cosine(positions * freq)
    source = lax.broadcasted_iota(jnp.int32, (HEAD, HEAD), 0)
    target = lax.broadcasted_iota(jnp.int32, (HEAD, HEAD), 1)
    partner = jnp.where(source == (target ^ 1), jnp.where((target & 1) == 0, 1.0, -1.0), 0.0).astype(jnp.bfloat16)
    half = out_ref.shape[2]
    for start in range(0, width, HEAD):
        size = min(HEAD, width - start)
        block = grad_ref[:, start : start + size]
        swapped = jnp.dot(block, partner[:size, :size], preferred_element_type=jnp.float32)
        turned = block.astype(jnp.float32) * cosine[:, :size] + swapped * sine[:, :size]
        columns = col_start + start + lax.broadcasted_iota(jnp.int32, (rows, size), 1)
        result = jnp.where(columns < ROTATED, turned, block.astype(jnp.float32)).astype(jnp.bfloat16)
        for copy in range(out_ref.shape[0]):
            for core in range(out_ref.shape[1]):
                out_ref[copy, core, :, start : start + size] = result[core * half : (core + 1) * half]


def unrotate(grad, positions, copies, cores):
    rows, width = grad.shape
    return pl.pallas_call(
        unrotate_kernel,
        out_shape=jax.ShapeDtypeStruct((copies, cores, rows // cores, width), jnp.bfloat16),
        in_specs=[pl.BlockSpec(memory_space=pltpu.VMEM)] * 2,
        out_specs=pl.BlockSpec(memory_space=pltpu.VMEM),
        name="unrotate",
    )(positions.reshape(1, rows), grad)


def arrange_kernel(arrived_ref, out_ref, parts_ref, sem):
    load = pltpu.make_async_copy(arrived_ref, parts_ref, sem)
    load.start()
    load.wait()
    width = parts_ref.shape[3]
    main = width // HEAD * HEAD
    rest = width - main
    yl, core = lax.axis_index("yl"), lax.axis_index("c")
    for far in range(2):
        for z4 in range(2):
            yh = (yl ^ far) * 2 + z4
            own = parts_ref[yh, core]
            other = parts_ref[yh, 1 - core]
            for copy in range(out_ref.shape[0]):
                out_ref[copy, far, z4, :, :main] = own[:, :main]
                out_ref[copy, far, z4, :, main : 2 * main] = other[:, :main]
                out_ref[copy, far, z4, :, 2 * main : 2 * main + rest] = own[:, main:]
                out_ref[copy, far, z4, :, 2 * main + rest :] = other[:, main:]


def arrange(parts, copies):
    tokens, width = parts.shape[2:]
    return pl.pallas_call(
        arrange_kernel,
        out_shape=jax.ShapeDtypeStruct((copies, 2, 2, tokens, 2 * width), jnp.bfloat16),
        in_specs=[pl.BlockSpec(memory_space=pl.ANY)],
        out_specs=pl.BlockSpec(memory_space=pltpu.VMEM),
        scratch_shapes=[pltpu.VMEM(parts.shape, parts.dtype), pltpu.SemaphoreType.DMA],
        compiler_params=pltpu.CompilerParams(vmem_limit_bytes=8 << 20),
        name="arrange",
    )(parts)


def total_of(grads_ref, own_ref, other_ref):
    groups, rows, width = grads_ref.shape
    main = own_ref.shape[0] // HEAD * HEAD
    last = jnp.concatenate([own_ref[main:], other_ref[main:]], axis=0)
    grads = grads_ref[...].reshape(groups * rows, width)
    total = jnp.dot(grads[:, :main], own_ref[:main], preferred_element_type=jnp.float32)
    total += jnp.dot(grads[:, main : 2 * main], other_ref[:main], preferred_element_type=jnp.float32)
    return total + jnp.dot(grads[:, 2 * main :], last, preferred_element_type=jnp.float32)


def load_part(arrived_ref, far, held_ref, sem):
    load = pltpu.make_async_copy(arrived_ref.at[:, far], held_ref, sem)
    load.start()
    load.wait()


def far_product_kernel(arrived_ref, own_ref, other_ref, out_ref, grads_ref, sem):
    @pl.when(pl.program_id(0) == 0)
    def _():
        load_part(arrived_ref, 1, grads_ref, sem)

    out_ref[...] = total_of(grads_ref, own_ref, other_ref).astype(out_ref.dtype)


def near_product_kernel(arrived_ref, own_ref, other_ref, added_ref, out_ref, grads_ref, sem):
    @pl.when(pl.program_id(0) == 0)
    def _():
        load_part(arrived_ref, 0, grads_ref, sem)

    total = total_of(grads_ref, own_ref, other_ref) + added_ref[...].astype(jnp.float32)
    out_ref[...] = total.astype(out_ref.dtype)


def input_product(grads, own_weight, other_weight, added=None):
    groups, _, rows, width = grads.shape
    columns, model = own_weight.shape
    by_column = lambda step: (0, step)
    weights = [pl.BlockSpec((columns, STEP), by_column)] * 2
    part = [pl.BlockSpec((groups * rows, STEP), by_column)]
    near = added is not None
    return pl.pallas_call(
        near_product_kernel if near else far_product_kernel,
        grid=(model // STEP,),
        out_shape=jax.ShapeDtypeStruct((groups * rows, model), jnp.bfloat16),
        in_specs=[pl.BlockSpec(memory_space=pl.ANY)] + weights + part * near,
        out_specs=part[0],
        scratch_shapes=[pltpu.VMEM((groups, rows, width), grads.dtype), pltpu.SemaphoreType.DMA],
        compiler_params=pltpu.CompilerParams(vmem_limit_bytes=12 << 20),
        cost_estimate=pl.CostEstimate(flops=2 * groups * rows * width * model, bytes_accessed=4 << 20, transcendentals=0),
        name="near_product" if near else "far_product",
    )(grads, own_weight, other_weight, *([added] * near))


def blocks_of(groups, size):
    own_yl = lax.axis_index("yl")
    for yl in range(2):
        for z4 in range(2):
            for group in range(groups):
                index = (yl * 2 + z4) * groups + group
                yield index, group, yl ^ own_yl, slice(z4 * size, (z4 + 1) * size)


def lend_kernel(arrived_ref, out_ref, grads_ref, sem):
    load = pltpu.make_async_copy(arrived_ref, grads_ref, sem)
    load.start()
    load.wait()
    groups, _, rows, width = grads_ref.shape
    columns = width // 2
    main = columns // HEAD * HEAD
    rest = columns - main
    half = rows // 2
    for index, group, far, place in blocks_of(groups, half):
        start = index * half
        lent = grads_ref[group, far, place]
        out_ref[start : start + half, :main] = lent[:, main : 2 * main]
        out_ref[start : start + half, main:columns] = lent[:, 2 * main + rest :]
    out_ref[:, columns:] = jnp.zeros_like(out_ref[:, columns:])


def lend(grads):
    groups, _, rows, width = grads.shape
    padded = pl.cdiv(width // 2, HEAD) * HEAD
    return pl.pallas_call(
        lend_kernel,
        out_shape=jax.ShapeDtypeStruct((2 * groups * rows, padded), grads.dtype),
        in_specs=[pl.BlockSpec(memory_space=pl.ANY)],
        out_specs=pl.BlockSpec(memory_space=pltpu.VMEM),
        scratch_shapes=[pltpu.VMEM(grads.shape, grads.dtype), pltpu.SemaphoreType.DMA],
        compiler_params=pltpu.CompilerParams(vmem_limit_bytes=8 << 20),
        name="lend",
    )(grads)


def weight_product_kernel(arrived_ref, lent_ref, inputs_ref, out_ref, grads_ref, held_ref, sem):
    groups, _, rows, width = grads_ref.shape
    columns = width // 2
    main = columns // HEAD * HEAD
    rest = columns - main
    half = rows // 2

    @pl.when(pl.program_id(0) == 0)
    def _():
        load = pltpu.make_async_copy(arrived_ref, grads_ref, sem)
        load.start()
        load.wait()
        core = lax.axis_index("c")
        for index, group, far, place in blocks_of(groups, half):
            own = pl.ds(pl.multiple_of((index * 2 + core) * half, half), half)
            other = pl.ds(pl.multiple_of((index * 2 + 1 - core) * half, half), half)
            held_ref[own, :main] = grads_ref[group, far, place, :main]
            held_ref[own, main:] = grads_ref[group, far, place, 2 * main : 2 * main + rest]
            held_ref[other] = lent_ref[index * half : (index + 1) * half, :columns]

    dims = (((0,), (0,)), ((), ()))
    out_ref[...] = lax.dot_general(held_ref[...], inputs_ref[...], dims, preferred_element_type=jnp.float32)


def weight_product(grads, lent, inputs):
    groups, _, rows, width = grads.shape
    columns, (tokens, model) = width // 2, inputs.shape
    by_column = lambda step: (0, step)
    return pl.pallas_call(
        weight_product_kernel,
        grid=(model // STEP,),
        out_shape=jax.ShapeDtypeStruct((columns, model), jnp.float32),
        in_specs=[
            pl.BlockSpec(memory_space=pl.ANY),
            pl.BlockSpec(lent.shape, lambda step: (0, 0)),
            pl.BlockSpec((tokens, STEP), by_column),
        ],
        out_specs=pl.BlockSpec((columns, STEP), by_column),
        scratch_shapes=[
            pltpu.VMEM(grads.shape, grads.dtype),
            pltpu.VMEM((tokens, columns), jnp.bfloat16),
            pltpu.SemaphoreType.DMA,
        ],
        compiler_params=pltpu.CompilerParams(vmem_limit_bytes=12 << 20),
        cost_estimate=pl.CostEstimate(flops=2 * tokens * columns * model, bytes_accessed=6 << 20, transcendentals=0),
        name="weight_product",
    )(grads, lent, inputs)


def exchange(parts, axes):
    return lax.all_to_all(parts, axes, 0, 0, tiled=True)


def swapped(array, axis):
    return lax.ppermute(array, axis, SWAP)


def per_device(inputs, weight, grad_out, positions):
    width = weight.shape[1]
    tokens, model = inputs.shape

    sent = unrotate(grad_out, positions, lax.axis_size("yh"), lax.axis_size("c"))
    sent, weight = lax.optimization_barrier((sent, weight))
    parts = exchange(sent.reshape(-1, tokens, width), ("yh", "c"))
    parts = arrange(parts.reshape(sent.shape), lax.axis_size("x"))
    grads = exchange(parts, "x").reshape(-1, 2, 2 * tokens, 2 * width)

    own_weight = weight.T
    other_weight = swapped(own_weight, "c")
    all_inputs = lax.all_gather(inputs, COL, axis=0, tiled=True)

    far = input_product(grads, own_weight, other_weight)
    later, _ = lax.optimization_barrier((grads, far))
    lent = swapped(lend(later), "c")
    near = input_product(grads, own_weight, other_weight, swapped(far, "yl"))
    parts = exchange(near.reshape(-1, tokens, model), ("z2", "z1", "z4"))
    weight_grad = weight_product(grads, lent, all_inputs).T
    parts, weight_grad = lax.optimization_barrier((parts, weight_grad))
    input_grad = parts.astype(jnp.float32).sum(axis=0).astype(jnp.bfloat16)
    return input_grad, weight_grad


def solution(mesh):
    sizes = {"yh": 4, "x": 4, "yl": 2, "z4": 2, "z2": 2, "z1": 2, "c": 2}
    finer = Mesh(mesh.devices.reshape(tuple(sizes.values())), tuple(sizes))
    in_specs = (P(COL, ROW), P(ROW, COL), P(ROW, COL), P(ROW))
    out_specs = (P(COL, ROW), P(ROW, COL))
    return jax.shard_map(per_device, mesh=finer, in_specs=in_specs, out_specs=out_specs, check_vma=False)
```

```python
import functools
import math

import jax
import jax.numpy as jnp
from jax import lax
from jax.experimental import pallas as pl
from jax.experimental.pallas import tpu as pltpu
from jax.sharding import Mesh, PartitionSpec as P

QHEADS = 128
KVHEADS = 8
HEAD = 128
ROTATED = (QHEADS + KVHEADS) * HEAD

HALF_PI = (1.5703125, 4.837512969970703e-4, 7.549789948768648e-8)
ROW = ("yh", "x")
COL = ("yl", "z4", "z2", "z1", "c")
SWAP = ((0, 1), (1, 0))
STEP = 256


def scaled_freq(within):
    base = jnp.exp(-(2.0 * within.astype(jnp.float32) / HEAD) * math.log(500000.0))
    wave = 2.0 * math.pi / base
    smooth = (8192.0 / wave - 1.0) / 3.0
    middle = (1.0 - smooth) * base / 8.0 + smooth * base
    return jnp.where(wave < 2048.0, base, jnp.where(wave > 8192.0, base / 8.0, middle))


def sine_cosine(angle):
    turns = jnp.floor(angle * (2.0 / math.pi) + 0.5)
    rest = angle
    for part in HALF_PI:
        rest = rest - turns * part
    square = rest * rest
    sine = rest + rest * square * (
        -1.6666654611e-1 + square * (8.3321608736e-3 + square * -1.9515295891e-4)
    )
    cosine = (
        1.0
        - 0.5 * square
        + square * square * (4.166664568298827e-2 + square * (-1.388731625493765e-3 + square * 2.443315711809948e-5))
    )
    quarter = turns.astype(jnp.int32)
    odd = (quarter & 1) == 1
    sine, cosine = jnp.where(odd, cosine, sine), jnp.where(odd, sine, cosine)
    sine = jnp.where((quarter & 2) == 2, -sine, sine)
    cosine = jnp.where(((quarter + 1) & 2) == 2, -cosine, cosine)
    return sine, cosine


def unrotate_kernel(positions_ref, grad_ref, out_ref):
    rows, width = grad_ref.shape
    col_start = lax.axis_index(COL) * width
    row = lax.broadcasted_iota(jnp.int32, (rows, rows), 0)
    column = lax.broadcasted_iota(jnp.int32, (rows, rows), 1)
    spread = jnp.where(row == column, positions_ref[...].astype(jnp.float32), 0.0)
    positions = jnp.sum(spread, axis=1, keepdims=True)
    lane = lax.broadcasted_iota(jnp.int32, (8, HEAD), 1)
    freq = scaled_freq(((col_start + lane) & (HEAD - 1)) >> 1)[:1]
    sine, cosine = sine_cosine(positions * freq)
    source = lax.broadcasted_iota(jnp.int32, (HEAD, HEAD), 0)
    target = lax.broadcasted_iota(jnp.int32, (HEAD, HEAD), 1)
    partner = jnp.where(source == (target ^ 1), jnp.where((target & 1) == 0, 1.0, -1.0), 0.0).astype(jnp.bfloat16)
    half = out_ref.shape[2]
    for start in range(0, width, HEAD):
        size = min(HEAD, width - start)
        block = grad_ref[:, start : start + size]
        swapped = jnp.dot(block, partner[:size, :size], preferred_element_type=jnp.float32)
        turned = block.astype(jnp.float32) * cosine[:, :size] + swapped * sine[:, :size]
        columns = col_start + start + lax.broadcasted_iota(jnp.int32, (rows, size), 1)
        result = jnp.where(columns < ROTATED, turned, block.astype(jnp.float32)).astype(jnp.bfloat16)
        for copy in range(out_ref.shape[0]):
            for core in range(out_ref.shape[1]):
                out_ref[copy, core, :, start : start + size] = result[core * half : (core + 1) * half]


def unrotate(grad, positions, copies, cores):
    rows, width = grad.shape
    return pl.pallas_call(
        unrotate_kernel,
        out_shape=jax.ShapeDtypeStruct((copies, cores, rows // cores, width), jnp.bfloat16),
        in_specs=[pl.BlockSpec(memory_space=pltpu.VMEM)] * 2,
        out_specs=pl.BlockSpec(memory_space=pltpu.VMEM),
        name="unrotate",
    )(positions.reshape(1, rows), grad)


def arrange_kernel(arrived_ref, out_ref, parts_ref, laid_ref, sem, out_sems):
    load = pltpu.make_async_copy(arrived_ref, parts_ref, sem)
    load.start()
    load.wait()
    width = parts_ref.shape[3]
    main = width // HEAD * HEAD
    rest = width - main
    yl, core = lax.axis_index("yl"), lax.axis_index("c")
    for far in range(2):
        for z4 in range(2):
            yh = (yl ^ far) * 2 + z4
            own = parts_ref[yh, core]
            other = parts_ref[yh, 1 - core]
            laid_ref[far, z4, :, :main] = own[:, :main]
            laid_ref[far, z4, :, main : 2 * main] = other[:, :main]
            laid_ref[far, z4, :, 2 * main : 2 * main + rest] = own[:, main:]
            laid_ref[far, z4, :, 2 * main + rest :] = other[:, main:]
    copies = [pltpu.make_async_copy(laid_ref, out_ref.at[i], out_sems.at[i]) for i in range(out_ref.shape[0])]
    for copy in copies:
        copy.start()
    for copy in copies:
        copy.wait()


def arrange(parts, copies):
    tokens, width = parts.shape[2:]
    return pl.pallas_call(
        arrange_kernel,
        out_shape=jax.ShapeDtypeStruct((copies, 2, 2, tokens, 2 * width), jnp.bfloat16),
        in_specs=[pl.BlockSpec(memory_space=pl.ANY)],
        out_specs=pl.BlockSpec(memory_space=pltpu.HBM),
        scratch_shapes=[
            pltpu.VMEM(parts.shape, parts.dtype),
            pltpu.VMEM((2, 2, tokens, 2 * width), parts.dtype),
            pltpu.SemaphoreType.DMA,
            pltpu.SemaphoreType.DMA((copies,)),
        ],
        compiler_params=pltpu.CompilerParams(vmem_limit_bytes=8 << 20),
        name="arrange",
    )(parts)


def total_of(grads_ref, own_ref, other_ref):
    groups, rows, width = grads_ref.shape
    main = own_ref.shape[0] // HEAD * HEAD
    last = jnp.concatenate([own_ref[main:], other_ref[main:]], axis=0)
    grads = grads_ref[...].reshape(groups * rows, width)
    total = jnp.dot(grads[:, :main], own_ref[:main], preferred_element_type=jnp.float32)
    total += jnp.dot(grads[:, main : 2 * main], other_ref[:main], preferred_element_type=jnp.float32)
    return total + jnp.dot(grads[:, 2 * main :], last, preferred_element_type=jnp.float32)


def load_part(arrived_ref, far, held_ref, sem):
    load = pltpu.make_async_copy(arrived_ref.at[:, far], held_ref, sem)
    load.start()
    load.wait()


def far_product_kernel(arrived_ref, own_ref, other_ref, out_ref, grads_ref, sem):
    @pl.when(pl.program_id(0) == 0)
    def _():
        load_part(arrived_ref, 1, grads_ref, sem)

    out_ref[...] = total_of(grads_ref, own_ref, other_ref).astype(out_ref.dtype)


def near_product_kernel(arrived_ref, own_ref, other_ref, added_ref, out_ref, grads_ref, sem, held_ref, out_sems):
    step = pl.program_id(0)

    @pl.when(step == 0)
    def _():
        load_part(arrived_ref, 0, grads_ref, sem)

    total = total_of(grads_ref, own_ref, other_ref) + added_ref[...].astype(jnp.float32)
    held_ref[step] = total.astype(held_ref.dtype)

    def store(at):
        return pltpu.make_async_copy(held_ref.at[at], out_ref.at[:, pl.ds(at * STEP, STEP)], out_sems.at[at])

    store(step).start()

    @pl.when(step == pl.num_programs(0) - 1)
    def _():
        for at in range(held_ref.shape[0]):
            store(at).wait()


def input_product(grads, own_weight, other_weight, added=None):
    groups, _, rows, width = grads.shape
    columns, model = own_weight.shape
    by_column = lambda step: (0, step)
    weights = [pl.BlockSpec((columns, STEP), by_column)] * 2
    part = [pl.BlockSpec((groups * rows, STEP), by_column)]
    near = added is not None
    steps = model // STEP
    store = [pltpu.VMEM((steps, groups * rows, STEP), jnp.bfloat16), pltpu.SemaphoreType.DMA((steps,))]
    return pl.pallas_call(
        near_product_kernel if near else far_product_kernel,
        grid=(model // STEP,),
        out_shape=jax.ShapeDtypeStruct((groups * rows, model), jnp.bfloat16),
        in_specs=[pl.BlockSpec(memory_space=pl.ANY)] + weights + part * near,
        out_specs=pl.BlockSpec(memory_space=pltpu.HBM) if near else part[0],
        scratch_shapes=[pltpu.VMEM((groups, rows, width), grads.dtype), pltpu.SemaphoreType.DMA] + store * near,
        compiler_params=pltpu.CompilerParams(vmem_limit_bytes=12 << 20),
        cost_estimate=pl.CostEstimate(flops=2 * groups * rows * width * model, bytes_accessed=4 << 20, transcendentals=0),
        name="near_product" if near else "far_product",
    )(grads, own_weight, other_weight, *([added] * near))


def blocks_of(groups, size):
    z1, z2, z4 = lax.axis_index("z1"), lax.axis_index("z2"), lax.axis_index("z4")
    for index in range(4 * groups):
        group = ((index >> 2 & 1) ^ z2) * 2 + ((index >> 3) ^ z1)
        place = pl.ds(pl.multiple_of(((index >> 1 & 1) ^ z4) * size, size), size)
        yield index * size, group, index & 1, place


def weight_product_kernel(side, arrived_ref, first_ref, second_ref, *refs):
    grads_ref, held_ref, sem = refs[-3:]
    groups, _, rows, width = grads_ref.shape
    columns = width // 2
    main = columns // HEAD * HEAD
    rest = columns - main
    half = rows // 2
    split = first_ref.shape[0]
    step = pl.program_id(0)
    early = step < pl.num_programs(0) // 2

    @pl.when(step == 0)
    def _():
        load = pltpu.make_async_copy(arrived_ref, grads_ref, sem)
        load.start()
        load.wait()
        for start, group, far, place in blocks_of(groups, half):
            held_ref[start : start + half, :main] = grads_ref[group, far, place, side * main : (side + 1) * main]
            last = 2 * main + side * rest
            held_ref[start : start + half, main:] = grads_ref[group, far, place, last : last + rest]

    dims = (((0,), (0,)), ((), ()))
    total = lax.dot_general(held_ref[:split], first_ref[...], dims, preferred_element_type=jnp.float32)
    total += lax.dot_general(held_ref[split:], second_ref[...], dims, preferred_element_type=jnp.float32)
    if side == 0:
        left_ref, right_ref, out_ref = refs[:3]
        out_ref[...] = total + jnp.where(early, left_ref[...], right_ref[...]).astype(jnp.float32)
    else:
        left_ref, right_ref = refs[:2]

        @pl.when(early)
        def _():
            left_ref[...] = total.astype(left_ref.dtype)

        @pl.when(jnp.logical_not(early))
        def _():
            right_ref[...] = total.astype(right_ref.dtype)


def weight_product(grads, first, second, added=None):
    width = grads.shape[3]
    columns, (tokens, model) = width // 2, first.shape
    steps = model // STEP
    by_column = lambda step: (0, step)
    whole = pl.BlockSpec((columns, STEP), by_column)
    left = pl.BlockSpec((columns, STEP), lambda step: (0, jnp.minimum(step, steps // 2 - 1)))
    right = pl.BlockSpec((columns, STEP), lambda step: (0, jnp.maximum(step - steps // 2, 0)))
    own = added is not None
    return pl.pallas_call(
        functools.partial(weight_product_kernel, 0 if own else 1),
        grid=(steps,),
        out_shape=jax.ShapeDtypeStruct((columns, model), jnp.float32)
        if own
        else [jax.ShapeDtypeStruct((columns, model // 2), jnp.bfloat16)] * 2,
        in_specs=[pl.BlockSpec(memory_space=pl.ANY)]
        + [pl.BlockSpec((tokens, STEP), by_column)] * 2
        + [left, right] * own,
        out_specs=whole if own else [left, right],
        scratch_shapes=[
            pltpu.VMEM(grads.shape, grads.dtype),
            pltpu.VMEM((2 * tokens, columns), jnp.bfloat16),
            pltpu.SemaphoreType.DMA,
        ],
        compiler_params=pltpu.CompilerParams(vmem_limit_bytes=16 << 20),
        cost_estimate=pl.CostEstimate(flops=4 * tokens * columns * model, bytes_accessed=6 << 20, transcendentals=0),
        name="own_weight_product" if own else "other_weight_product",
    )(grads, first, second, *(added if own else ()))


def exchange(parts, axes):
    return lax.all_to_all(parts, axes, 0, 0, tiled=True)


def swapped(array, axis):
    return lax.ppermute(array, axis, SWAP)


def after(array, earlier):
    return lax.optimization_barrier((array, earlier))[0]


def doubled(array, axis):
    return jnp.concatenate([array, swapped(array, axis)], 0)


def per_device(inputs, weight, grad_out, positions):
    width = weight.shape[1]
    tokens, model = inputs.shape

    sent = unrotate(grad_out, positions, lax.axis_size("yh"), lax.axis_size("c"))
    own_weight = weight.T
    own_inputs = doubled(after(inputs, sent), "yl")
    arrived = exchange(sent.reshape(-1, tokens, width), ("yh", "c"))
    arrived = after(arrived, own_inputs)
    parts = arrange(arrived.reshape(sent.shape), lax.axis_size("x"))
    other_weight = swapped(after(own_weight, sent), "c")
    own_inputs = doubled(after(own_inputs, parts), "z4")
    grads = exchange(parts, "x").reshape(-1, 2, 2 * tokens, 2 * width)
    own_inputs = doubled(own_inputs, "z2")

    far = input_product(grads, own_weight, other_weight)
    own_inputs = after(own_inputs, far)
    second = swapped(own_inputs, "z1")
    near = input_product(grads, own_weight, other_weight, swapped(far, "yl"))
    parts = exchange(near.reshape(-1, tokens, model), ("z2", "z1", "z4"))
    second = after(second, near)
    lent = [swapped(half, "c") for half in weight_product(grads, own_inputs, second)]
    weight_grad = weight_product(grads, own_inputs, second, lent).T
    parts, weight_grad = lax.optimization_barrier((parts, weight_grad))
    input_grad = parts.astype(jnp.float32).sum(axis=0).astype(jnp.bfloat16)
    return input_grad, weight_grad


def solution(mesh):
    sizes = {"yh": 4, "x": 4, "yl": 2, "z4": 2, "z2": 2, "z1": 2, "c": 2}
    finer = Mesh(mesh.devices.reshape(tuple(sizes.values())), tuple(sizes))
    in_specs = (P(COL, ROW), P(ROW, COL), P(ROW, COL), P(ROW))
    out_specs = (P(COL, ROW), P(ROW, COL))
    return jax.shard_map(per_device, mesh=finer, in_specs=in_specs, out_specs=out_specs, check_vma=False)
```

```python
import functools
import math

import jax
import jax.numpy as jnp
from jax import lax
from jax.experimental import pallas as pl
from jax.experimental.pallas import tpu as pltpu
from jax.sharding import Mesh, PartitionSpec as P

QHEADS = 128
KVHEADS = 8
HEAD = 128
ROTATED = (QHEADS + KVHEADS) * HEAD

HALF_PI = (1.5703125, 4.837512969970703e-4, 7.549789948768648e-8)
ROW = ("yh", "x")
COL = ("yl", "z4", "z2", "z1", "c")
SWAP = ((0, 1), (1, 0))
STEP = 512
WIDE = 512


def scaled_freq(within):
    base = jnp.exp(-(2.0 * within.astype(jnp.float32) / HEAD) * math.log(500000.0))
    wave = 2.0 * math.pi / base
    smooth = (8192.0 / wave - 1.0) / 3.0
    middle = (1.0 - smooth) * base / 8.0 + smooth * base
    return jnp.where(wave < 2048.0, base, jnp.where(wave > 8192.0, base / 8.0, middle))


def sine_cosine(angle):
    turns = jnp.floor(angle * (2.0 / math.pi) + 0.5)
    rest = angle
    for part in HALF_PI:
        rest = rest - turns * part
    square = rest * rest
    sine = rest + rest * square * (
        -1.6666654611e-1 + square * (8.3321608736e-3 + square * -1.9515295891e-4)
    )
    cosine = (
        1.0
        - 0.5 * square
        + square * square * (4.166664568298827e-2 + square * (-1.388731625493765e-3 + square * 2.443315711809948e-5))
    )
    quarter = turns.astype(jnp.int32)
    odd = (quarter & 1) == 1
    sine, cosine = jnp.where(odd, cosine, sine), jnp.where(odd, sine, cosine)
    sine = jnp.where((quarter & 2) == 2, -sine, sine)
    cosine = jnp.where(((quarter + 1) & 2) == 2, -cosine, cosine)
    return sine, cosine


def unrotate_kernel(positions_ref, grad_ref, out_ref):
    rows, width = grad_ref.shape
    col_start = lax.axis_index(COL) * width
    row = lax.broadcasted_iota(jnp.int32, (rows, rows), 0)
    column = lax.broadcasted_iota(jnp.int32, (rows, rows), 1)
    spread = jnp.where(row == column, positions_ref[...].astype(jnp.float32), 0.0)
    positions = jnp.sum(spread, axis=1, keepdims=True)
    lane = lax.broadcasted_iota(jnp.int32, (8, HEAD), 1)
    freq = scaled_freq(((col_start + lane) & (HEAD - 1)) >> 1)[:1]
    sine, cosine = sine_cosine(positions * freq)
    source = lax.broadcasted_iota(jnp.int32, (HEAD, HEAD), 0)
    target = lax.broadcasted_iota(jnp.int32, (HEAD, HEAD), 1)
    partner = jnp.where(source == (target ^ 1), jnp.where((target & 1) == 0, 1.0, -1.0), 0.0).astype(jnp.bfloat16)
    half = out_ref.shape[2]
    for start in range(0, width, HEAD):
        size = min(HEAD, width - start)
        block = grad_ref[:, start : start + size]
        swapped = jnp.dot(block, partner[:size, :size], preferred_element_type=jnp.float32)
        turned = block.astype(jnp.float32) * cosine[:, :size] + swapped * sine[:, :size]
        columns = col_start + start + lax.broadcasted_iota(jnp.int32, (rows, size), 1)
        result = jnp.where(columns < ROTATED, turned, block.astype(jnp.float32)).astype(jnp.bfloat16)
        for copy in range(out_ref.shape[0]):
            for core in range(out_ref.shape[1]):
                out_ref[copy, core, :, start : start + size] = result[core * half : (core + 1) * half]


def unrotate(grad, positions, copies, cores):
    rows, width = grad.shape
    return pl.pallas_call(
        unrotate_kernel,
        out_shape=jax.ShapeDtypeStruct((copies, cores, rows // cores, width), jnp.bfloat16),
        in_specs=[pl.BlockSpec(memory_space=pltpu.VMEM)] * 2,
        out_specs=pl.BlockSpec(memory_space=pltpu.VMEM),
        name="unrotate",
    )(positions.reshape(1, rows), grad)


def arrange_kernel(arrived_ref, out_ref, parts_ref, laid_ref, sem, out_sems):
    load = pltpu.make_async_copy(arrived_ref, parts_ref, sem)
    load.start()
    load.wait()
    width = parts_ref.shape[3]
    main = width // HEAD * HEAD
    rest = width - main
    yl, core = lax.axis_index("yl"), lax.axis_index("c")
    for far in range(2):
        for z4 in range(2):
            yh = (yl ^ far) * 2 + z4
            own = parts_ref[yh, core]
            other = parts_ref[yh, 1 - core]
            laid_ref[far, z4, :, :main] = own[:, :main]
            laid_ref[far, z4, :, main : 2 * main] = other[:, :main]
            laid_ref[far, z4, :, 2 * main : 2 * main + rest] = own[:, main:]
            laid_ref[far, z4, :, 2 * main + rest :] = other[:, main:]
    copies = [pltpu.make_async_copy(laid_ref, out_ref.at[i], out_sems.at[i]) for i in range(out_ref.shape[0])]
    for copy in copies:
        copy.start()
    for copy in copies:
        copy.wait()


def arrange(parts, copies):
    tokens, width = parts.shape[2:]
    return pl.pallas_call(
        arrange_kernel,
        out_shape=jax.ShapeDtypeStruct((copies, 2, 2, tokens, 2 * width), jnp.bfloat16),
        in_specs=[pl.BlockSpec(memory_space=pl.ANY)],
        out_specs=pl.BlockSpec(memory_space=pltpu.HBM),
        scratch_shapes=[
            pltpu.VMEM(parts.shape, parts.dtype),
            pltpu.VMEM((2, 2, tokens, 2 * width), parts.dtype),
            pltpu.SemaphoreType.DMA,
            pltpu.SemaphoreType.DMA((copies,)),
        ],
        compiler_params=pltpu.CompilerParams(vmem_limit_bytes=8 << 20),
        name="arrange",
    )(parts)


def total_of(grads_ref, own_ref, other_ref):
    groups, rows, width = grads_ref.shape
    main = own_ref.shape[0] // HEAD * HEAD
    last = jnp.concatenate([own_ref[main:], other_ref[main:]], axis=0)
    grads = grads_ref[...].reshape(groups * rows, width)
    total = jnp.dot(grads[:, :main], own_ref[:main], preferred_element_type=jnp.float32)
    total += jnp.dot(grads[:, main : 2 * main], other_ref[:main], preferred_element_type=jnp.float32)
    return total + jnp.dot(grads[:, 2 * main :], last, preferred_element_type=jnp.float32)


def load_part(arrived_ref, far, held_ref, sem):
    load = pltpu.make_async_copy(arrived_ref.at[:, far], held_ref, sem)
    load.start()
    load.wait()


def far_product_kernel(arrived_ref, own_ref, other_ref, out_ref, grads_ref, sem):
    @pl.when(pl.program_id(0) == 0)
    def _():
        load_part(arrived_ref, 1, grads_ref, sem)

    out_ref[...] = total_of(grads_ref, own_ref, other_ref).astype(out_ref.dtype)


def near_product_kernel(arrived_ref, own_ref, other_ref, added_ref, out_ref, grads_ref, sem, held_ref, out_sems):
    step = pl.program_id(0)

    @pl.when(step == 0)
    def _():
        load_part(arrived_ref, 0, grads_ref, sem)

    total = total_of(grads_ref, own_ref, other_ref) + added_ref[...].astype(jnp.float32)
    held_ref[step] = total.astype(held_ref.dtype)

    def store(at):
        return pltpu.make_async_copy(held_ref.at[at], out_ref.at[:, pl.ds(at * STEP, STEP)], out_sems.at[at])

    store(step).start()

    @pl.when(step == pl.num_programs(0) - 1)
    def _():
        for at in range(held_ref.shape[0]):
            store(at).wait()


def input_product(grads, own_weight, other_weight, added=None):
    groups, _, rows, width = grads.shape
    columns, model = own_weight.shape
    by_column = lambda step: (0, step)
    weights = [pl.BlockSpec((columns, STEP), by_column)] * 2
    part = [pl.BlockSpec((groups * rows, STEP), by_column)]
    near = added is not None
    steps = model // STEP
    store = [pltpu.VMEM((steps, groups * rows, STEP), jnp.bfloat16), pltpu.SemaphoreType.DMA((steps,))]
    return pl.pallas_call(
        near_product_kernel if near else far_product_kernel,
        grid=(model // STEP,),
        out_shape=jax.ShapeDtypeStruct((groups * rows, model), jnp.bfloat16),
        in_specs=[pl.BlockSpec(memory_space=pl.ANY)] + weights + part * near,
        out_specs=pl.BlockSpec(memory_space=pltpu.HBM) if near else part[0],
        scratch_shapes=[pltpu.VMEM((groups, rows, width), grads.dtype), pltpu.SemaphoreType.DMA] + store * near,
        compiler_params=pltpu.CompilerParams(vmem_limit_bytes=12 << 20),
        cost_estimate=pl.CostEstimate(flops=2 * groups * rows * width * model, bytes_accessed=4 << 20, transcendentals=0),
        name="near_product" if near else "far_product",
    )(grads, own_weight, other_weight, *([added] * near))


def blocks_of(groups, size):
    z1, z2, z4 = lax.axis_index("z1"), lax.axis_index("z2"), lax.axis_index("z4")
    for index in range(4 * groups):
        group = ((index >> 2 & 1) ^ z2) * 2 + ((index >> 3) ^ z1)
        place = pl.ds(pl.multiple_of(((index >> 1 & 1) ^ z4) * size, size), size)
        yield index * size, group, index & 1, place


def weight_product_kernel(side, arrived_ref, first_ref, second_ref, *refs):
    grads_ref, held_ref, turned_ref, sem = refs[-4:]
    groups, _, rows, width = grads_ref.shape
    columns = width // 2
    main = columns // HEAD * HEAD
    rest = columns - main
    half = rows // 2
    split = first_ref.shape[0]
    step = pl.program_id(0)
    early = step < pl.num_programs(0) // 2

    @pl.when(step == 0)
    def _():
        load = pltpu.make_async_copy(arrived_ref, grads_ref, sem)
        load.start()
        load.wait()
        for start, group, far, place in blocks_of(groups, half):
            held_ref[start : start + half, :main] = grads_ref[group, far, place, side * main : (side + 1) * main]
            last = 2 * main + side * rest
            held_ref[start : start + half, main:columns] = grads_ref[group, far, place, last : last + rest]
        held_ref[:, columns:] = jnp.zeros_like(held_ref[:, columns:])
        turned_ref[...] = held_ref[...].T

    total = jnp.dot(turned_ref[:columns, :split], first_ref[...], preferred_element_type=jnp.float32)
    total += jnp.dot(turned_ref[:columns, split:], second_ref[...], preferred_element_type=jnp.float32)
    if side == 0:
        left_ref, right_ref, out_ref = refs[:3]
        out_ref[...] = total + jnp.where(early, left_ref[...], right_ref[...]).astype(jnp.float32)
    else:
        left_ref, right_ref = refs[:2]

        @pl.when(early)
        def _():
            left_ref[...] = total.astype(left_ref.dtype)

        @pl.when(jnp.logical_not(early))
        def _():
            right_ref[...] = total.astype(right_ref.dtype)


def weight_product(grads, first, second, added=None):
    width = grads.shape[3]
    columns, (tokens, model) = width // 2, first.shape
    padded = pl.cdiv(columns, HEAD) * HEAD
    steps = model // WIDE
    by_column = lambda step: (0, step)
    whole = pl.BlockSpec((columns, WIDE), by_column)
    left = pl.BlockSpec((columns, WIDE), lambda step: (0, jnp.minimum(step, steps // 2 - 1)))
    right = pl.BlockSpec((columns, WIDE), lambda step: (0, jnp.maximum(step - steps // 2, 0)))
    own = added is not None
    return pl.pallas_call(
        functools.partial(weight_product_kernel, 0 if own else 1),
        grid=(steps,),
        out_shape=jax.ShapeDtypeStruct((columns, model), jnp.float32)
        if own
        else [jax.ShapeDtypeStruct((columns, model // 2), jnp.bfloat16)] * 2,
        in_specs=[pl.BlockSpec(memory_space=pl.ANY)]
        + [pl.BlockSpec((tokens, WIDE), by_column)] * 2
        + [left, right] * own,
        out_specs=whole if own else [left, right],
        scratch_shapes=[
            pltpu.VMEM(grads.shape, grads.dtype),
            pltpu.VMEM((2 * tokens, padded), jnp.bfloat16),
            pltpu.VMEM((padded, 2 * tokens), jnp.bfloat16),
            pltpu.SemaphoreType.DMA,
        ],
        compiler_params=pltpu.CompilerParams(vmem_limit_bytes=24 << 20),
        cost_estimate=pl.CostEstimate(flops=4 * tokens * columns * model, bytes_accessed=6 << 20, transcendentals=0),
        name="own_weight_product" if own else "other_weight_product",
    )(grads, first, second, *(added if own else ()))


def exchange(parts, axes):
    return lax.all_to_all(parts, axes, 0, 0, tiled=True)


def swapped(array, axis):
    return lax.ppermute(array, axis, SWAP)


def after(array, earlier):
    return lax.optimization_barrier((array, earlier))[0]


def doubled(array, axis):
    return jnp.concatenate([array, swapped(array, axis)], 0)


def per_device(inputs, weight, grad_out, positions):
    width = weight.shape[1]
    tokens, model = inputs.shape

    sent = unrotate(grad_out, positions, lax.axis_size("yh"), lax.axis_size("c"))
    own_weight = weight.T
    own_inputs = doubled(after(inputs, sent), "yl")
    arrived = exchange(sent.reshape(-1, tokens, width), ("yh", "c"))
    arrived = after(arrived, own_inputs)
    parts = arrange(arrived.reshape(sent.shape), lax.axis_size("x"))
    own_inputs = doubled(own_inputs, "z4")
    other_weight = swapped(after(own_weight, sent), "c")
    grads = exchange(parts, "x").reshape(-1, 2, 2 * tokens, 2 * width)
    own_inputs = doubled(own_inputs, "z2")

    far = input_product(grads, own_weight, other_weight)
    own_inputs = after(own_inputs, far)
    second = swapped(own_inputs, "z1")
    near = input_product(grads, own_weight, other_weight, swapped(far, "yl"))
    parts = exchange(near.reshape(-1, tokens, model), ("z2", "z1", "z4"))
    second = after(second, near)
    lent = [swapped(half, "c") for half in weight_product(grads, own_inputs, second)]
    weight_grad = weight_product(grads, own_inputs, second, lent).T
    parts, weight_grad = lax.optimization_barrier((parts, weight_grad))
    input_grad = parts.astype(jnp.float32).sum(axis=0).astype(jnp.bfloat16)
    return input_grad, weight_grad


def solution(mesh):
    sizes = {"yh": 4, "x": 4, "yl": 2, "z4": 2, "z2": 2, "z1": 2, "c": 2}
    finer = Mesh(mesh.devices.reshape(tuple(sizes.values())), tuple(sizes))
    in_specs = (P(COL, ROW), P(ROW, COL), P(ROW, COL), P(ROW))
    out_specs = (P(COL, ROW), P(ROW, COL))
    return jax.shard_map(per_device, mesh=finer, in_specs=in_specs, out_specs=out_specs, check_vma=False)
```

```python
import functools
import math

import jax
import jax.numpy as jnp
from jax import lax
from jax.experimental import pallas as pl
from jax.experimental.pallas import tpu as pltpu
from jax.sharding import Mesh, PartitionSpec as P

QHEADS = 128
KVHEADS = 8
HEAD = 128
ROTATED = (QHEADS + KVHEADS) * HEAD

HALF_PI = (1.5703125, 4.837512969970703e-4, 7.549789948768648e-8)
ROW = ("yh", "x")
COL = ("yl", "z4", "z2", "z1", "c")
SWAP = ((0, 1), (1, 0))
STEP = 256
WIDE = 512


def scaled_freq(within):
    base = jnp.exp(-(2.0 * within.astype(jnp.float32) / HEAD) * math.log(500000.0))
    wave = 2.0 * math.pi / base
    smooth = (8192.0 / wave - 1.0) / 3.0
    middle = (1.0 - smooth) * base / 8.0 + smooth * base
    return jnp.where(wave < 2048.0, base, jnp.where(wave > 8192.0, base / 8.0, middle))


def sine_cosine(angle):
    turns = jnp.floor(angle * (2.0 / math.pi) + 0.5)
    rest = angle
    for part in HALF_PI:
        rest = rest - turns * part
    square = rest * rest
    sine = rest + rest * square * (
        -1.6666654611e-1 + square * (8.3321608736e-3 + square * -1.9515295891e-4)
    )
    cosine = (
        1.0
        - 0.5 * square
        + square * square * (4.166664568298827e-2 + square * (-1.388731625493765e-3 + square * 2.443315711809948e-5))
    )
    quarter = turns.astype(jnp.int32)
    odd = (quarter & 1) == 1
    sine, cosine = jnp.where(odd, cosine, sine), jnp.where(odd, sine, cosine)
    sine = jnp.where((quarter & 2) == 2, -sine, sine)
    cosine = jnp.where(((quarter + 1) & 2) == 2, -cosine, cosine)
    return sine, cosine


def unrotate_kernel(positions_ref, grad_ref, out_ref):
    rows, width = grad_ref.shape
    col_start = lax.axis_index(COL) * width
    row = lax.broadcasted_iota(jnp.int32, (rows, rows), 0)
    column = lax.broadcasted_iota(jnp.int32, (rows, rows), 1)
    spread = jnp.where(row == column, positions_ref[...].astype(jnp.float32), 0.0)
    positions = jnp.sum(spread, axis=1, keepdims=True)
    lane = lax.broadcasted_iota(jnp.int32, (8, HEAD), 1)
    freq = scaled_freq(((col_start + lane) & (HEAD - 1)) >> 1)[:1]
    sine, cosine = sine_cosine(positions * freq)
    source = lax.broadcasted_iota(jnp.int32, (HEAD, HEAD), 0)
    target = lax.broadcasted_iota(jnp.int32, (HEAD, HEAD), 1)
    partner = jnp.where(source == (target ^ 1), jnp.where((target & 1) == 0, 1.0, -1.0), 0.0).astype(jnp.bfloat16)
    half = out_ref.shape[2]
    for start in range(0, width, HEAD):
        size = min(HEAD, width - start)
        block = grad_ref[:, start : start + size]
        swapped = jnp.dot(block, partner[:size, :size], preferred_element_type=jnp.float32)
        turned = block.astype(jnp.float32) * cosine[:, :size] + swapped * sine[:, :size]
        columns = col_start + start + lax.broadcasted_iota(jnp.int32, (rows, size), 1)
        result = jnp.where(columns < ROTATED, turned, block.astype(jnp.float32)).astype(jnp.bfloat16)
        for copy in range(out_ref.shape[0]):
            for core in range(out_ref.shape[1]):
                out_ref[copy, core, :, start : start + size] = result[core * half : (core + 1) * half]


def unrotate(grad, positions, copies, cores):
    rows, width = grad.shape
    return pl.pallas_call(
        unrotate_kernel,
        out_shape=jax.ShapeDtypeStruct((copies, cores, rows // cores, width), jnp.bfloat16),
        in_specs=[pl.BlockSpec(memory_space=pltpu.VMEM)] * 2,
        out_specs=pl.BlockSpec(memory_space=pltpu.VMEM),
        name="unrotate",
    )(positions.reshape(1, rows), grad)


def arrange_kernel(arrived_ref, out_ref, parts_ref, laid_ref, sem, out_sems):
    load = pltpu.make_async_copy(arrived_ref, parts_ref, sem)
    load.start()
    load.wait()
    width = parts_ref.shape[3]
    main = width // HEAD * HEAD
    rest = width - main
    yl, core = lax.axis_index("yl"), lax.axis_index("c")
    for far in range(2):
        for z4 in range(2):
            yh = (yl ^ far) * 2 + z4
            own = parts_ref[yh, core]
            other = parts_ref[yh, 1 - core]
            laid_ref[far, z4, :, :main] = own[:, :main]
            laid_ref[far, z4, :, main : 2 * main] = other[:, :main]
            laid_ref[far, z4, :, 2 * main : 2 * main + rest] = own[:, main:]
            laid_ref[far, z4, :, 2 * main + rest :] = other[:, main:]
    copies = [pltpu.make_async_copy(laid_ref, out_ref.at[i], out_sems.at[i]) for i in range(out_ref.shape[0])]
    for copy in copies:
        copy.start()
    for copy in copies:
        copy.wait()


def arrange(parts, copies):
    tokens, width = parts.shape[2:]
    return pl.pallas_call(
        arrange_kernel,
        out_shape=jax.ShapeDtypeStruct((copies, 2, 2, tokens, 2 * width), jnp.bfloat16),
        in_specs=[pl.BlockSpec(memory_space=pl.ANY)],
        out_specs=pl.BlockSpec(memory_space=pltpu.HBM),
        scratch_shapes=[
            pltpu.VMEM(parts.shape, parts.dtype),
            pltpu.VMEM((2, 2, tokens, 2 * width), parts.dtype),
            pltpu.SemaphoreType.DMA,
            pltpu.SemaphoreType.DMA((copies,)),
        ],
        compiler_params=pltpu.CompilerParams(vmem_limit_bytes=8 << 20),
        name="arrange",
    )(parts)


def total_of(grads_ref, own_ref, other_ref):
    groups, rows, width = grads_ref.shape
    main = own_ref.shape[0] // HEAD * HEAD
    last = jnp.concatenate([own_ref[main:], other_ref[main:]], axis=0)
    grads = grads_ref[...].reshape(groups * rows, width)
    total = jnp.dot(grads[:, :main], own_ref[:main], preferred_element_type=jnp.float32)
    total += jnp.dot(grads[:, main : 2 * main], other_ref[:main], preferred_element_type=jnp.float32)
    return total + jnp.dot(grads[:, 2 * main :], last, preferred_element_type=jnp.float32)


def load_part(arrived_ref, far, held_ref, sem):
    load = pltpu.make_async_copy(arrived_ref.at[:, far], held_ref, sem)
    load.start()
    load.wait()


def far_product_kernel(arrived_ref, own_ref, other_ref, out_ref, grads_ref, sem):
    @pl.when(pl.program_id(0) == 0)
    def _():
        load_part(arrived_ref, 1, grads_ref, sem)

    out_ref[...] = total_of(grads_ref, own_ref, other_ref).astype(out_ref.dtype)


def near_product_kernel(arrived_ref, own_ref, other_ref, added_ref, out_ref, grads_ref, sem, held_ref, out_sems):
    step = pl.program_id(0)

    @pl.when(step == 0)
    def _():
        load_part(arrived_ref, 0, grads_ref, sem)

    total = total_of(grads_ref, own_ref, other_ref) + added_ref[...].astype(jnp.float32)
    held_ref[step] = total.astype(held_ref.dtype)

    def store(at):
        return pltpu.make_async_copy(held_ref.at[at], out_ref.at[:, pl.ds(at * STEP, STEP)], out_sems.at[at])

    store(step).start()

    @pl.when(step == pl.num_programs(0) - 1)
    def _():
        for at in range(held_ref.shape[0]):
            store(at).wait()


def input_product(grads, own_weight, other_weight, added=None):
    groups, _, rows, width = grads.shape
    columns, model = own_weight.shape
    by_column = lambda step: (0, step)
    weights = [pl.BlockSpec((columns, STEP), by_column)] * 2
    part = [pl.BlockSpec((groups * rows, STEP), by_column)]
    near = added is not None
    steps = model // STEP
    store = [pltpu.VMEM((steps, groups * rows, STEP), jnp.bfloat16), pltpu.SemaphoreType.DMA((steps,))]
    return pl.pallas_call(
        near_product_kernel if near else far_product_kernel,
        grid=(model // STEP,),
        out_shape=jax.ShapeDtypeStruct((groups * rows, model), jnp.bfloat16),
        in_specs=[pl.BlockSpec(memory_space=pl.ANY)] + weights + part * near,
        out_specs=pl.BlockSpec(memory_space=pltpu.HBM) if near else part[0],
        scratch_shapes=[pltpu.VMEM((groups, rows, width), grads.dtype), pltpu.SemaphoreType.DMA] + store * near,
        compiler_params=pltpu.CompilerParams(vmem_limit_bytes=12 << 20),
        cost_estimate=pl.CostEstimate(flops=2 * groups * rows * width * model, bytes_accessed=4 << 20, transcendentals=0),
        name="near_product" if near else "far_product",
    )(grads, own_weight, other_weight, *([added] * near))


def blocks_of(groups, size):
    z1, z2, z4 = lax.axis_index("z1"), lax.axis_index("z2"), lax.axis_index("z4")
    for index in range(4 * groups):
        group = ((index >> 2 & 1) ^ z2) * 2 + ((index >> 3) ^ z1)
        place = pl.ds(pl.multiple_of(((index >> 1 & 1) ^ z4) * size, size), size)
        yield index * size, group, index & 1, place


def weight_product_kernel(side, arrived_ref, first_ref, second_ref, *refs):
    grads_ref, held_ref, turned_ref, sem = refs[-4:]
    groups, _, rows, width = grads_ref.shape
    columns = width // 2
    main = columns // HEAD * HEAD
    rest = columns - main
    half = rows // 2
    split = first_ref.shape[0]
    step = pl.program_id(0)
    early = step < pl.num_programs(0) // 2

    @pl.when(step == 0)
    def _():
        load = pltpu.make_async_copy(arrived_ref, grads_ref, sem)
        load.start()
        load.wait()
        for start, group, far, place in blocks_of(groups, half):
            held_ref[start : start + half, :main] = grads_ref[group, far, place, side * main : (side + 1) * main]
            last = 2 * main + side * rest
            held_ref[start : start + half, main:columns] = grads_ref[group, far, place, last : last + rest]
        held_ref[:, columns:] = jnp.zeros_like(held_ref[:, columns:])
        turned_ref[...] = held_ref[...].T

    total = jnp.dot(turned_ref[:columns, :split], first_ref[...], preferred_element_type=jnp.float32)
    total += jnp.dot(turned_ref[:columns, split:], second_ref[...], preferred_element_type=jnp.float32)
    if side == 0:
        left_ref, right_ref, out_ref = refs[:3]
        out_ref[...] = total + jnp.where(early, left_ref[...], right_ref[...]).astype(jnp.float32)
    else:
        left_ref, right_ref = refs[:2]

        @pl.when(early)
        def _():
            left_ref[...] = total.astype(left_ref.dtype)

        @pl.when(jnp.logical_not(early))
        def _():
            right_ref[...] = total.astype(right_ref.dtype)


def weight_product(grads, first, second, added=None):
    width = grads.shape[3]
    columns, (tokens, model) = width // 2, first.shape
    padded = pl.cdiv(columns, HEAD) * HEAD
    steps = model // WIDE
    by_column = lambda step: (0, step)
    whole = pl.BlockSpec((columns, WIDE), by_column)
    left = pl.BlockSpec((columns, WIDE), lambda step: (0, jnp.minimum(step, steps // 2 - 1)))
    right = pl.BlockSpec((columns, WIDE), lambda step: (0, jnp.maximum(step - steps // 2, 0)))
    own = added is not None
    return pl.pallas_call(
        functools.partial(weight_product_kernel, 0 if own else 1),
        grid=(steps,),
        out_shape=jax.ShapeDtypeStruct((columns, model), jnp.float32)
        if own
        else [jax.ShapeDtypeStruct((columns, model // 2), jnp.bfloat16)] * 2,
        in_specs=[pl.BlockSpec(memory_space=pl.ANY)]
        + [pl.BlockSpec((tokens, WIDE), by_column)] * 2
        + [left, right] * own,
        out_specs=whole if own else [left, right],
        scratch_shapes=[
            pltpu.VMEM(grads.shape, grads.dtype),
            pltpu.VMEM((2 * tokens, padded), jnp.bfloat16),
            pltpu.VMEM((padded, 2 * tokens), jnp.bfloat16),
            pltpu.SemaphoreType.DMA,
        ],
        compiler_params=pltpu.CompilerParams(vmem_limit_bytes=24 << 20),
        cost_estimate=pl.CostEstimate(flops=4 * tokens * columns * model, bytes_accessed=6 << 20, transcendentals=0),
        name="own_weight_product" if own else "other_weight_product",
    )(grads, first, second, *(added if own else ()))


def exchange(parts, axes):
    return lax.all_to_all(parts, axes, 0, 0, tiled=True)


def swapped(array, axis):
    return lax.ppermute(array, axis, SWAP)


def after(array, earlier):
    return lax.optimization_barrier((array, earlier))[0]


def doubled(array, axis):
    return jnp.concatenate([array, swapped(array, axis)], 0)


def per_device(inputs, weight, grad_out, positions):
    width = weight.shape[1]
    tokens, model = inputs.shape

    sent = unrotate(grad_out, positions, lax.axis_size("yh"), lax.axis_size("c"))
    own_weight = weight.T
    own_inputs = doubled(after(inputs, sent), "yl")
    arrived = exchange(sent.reshape(-1, tokens, width), ("yh", "c"))
    arrived = after(arrived, own_inputs)
    parts = arrange(arrived.reshape(sent.shape), lax.axis_size("x"))
    other_weight = swapped(after(own_weight, sent), "c")
    own_inputs = doubled(after(own_inputs, parts), "z4")
    grads = exchange(parts, "x").reshape(-1, 2, 2 * tokens, 2 * width)
    own_inputs = doubled(own_inputs, "z2")

    far = input_product(grads, own_weight, other_weight)
    own_inputs = after(own_inputs, far)
    second = swapped(own_inputs, "z1")
    near = input_product(grads, own_weight, other_weight, swapped(far, "yl"))
    parts = exchange(near.reshape(-1, tokens, model), ("z2", "z1", "z4"))
    second = after(second, near)
    lent = [swapped(half, "c") for half in weight_product(grads, own_inputs, second)]
    weight_grad = weight_product(grads, own_inputs, second, lent).T
    parts, weight_grad = lax.optimization_barrier((parts, weight_grad))
    input_grad = parts.astype(jnp.float32).sum(axis=0).astype(jnp.bfloat16)
    return input_grad, weight_grad


def solution(mesh):
    sizes = {"yh": 4, "x": 4, "yl": 2, "z4": 2, "z2": 2, "z1": 2, "c": 2}
    finer = Mesh(mesh.devices.reshape(tuple(sizes.values())), tuple(sizes))
    in_specs = (P(COL, ROW), P(ROW, COL), P(ROW, COL), P(ROW))
    out_specs = (P(COL, ROW), P(ROW, COL))
    return jax.shard_map(per_device, mesh=finer, in_specs=in_specs, out_specs=out_specs, check_vma=False)
```

```python
import functools
import math

import jax
import jax.numpy as jnp
from jax import lax
from jax.experimental import pallas as pl
from jax.experimental.pallas import tpu as pltpu
from jax.sharding import Mesh, PartitionSpec as P

QHEADS = 128
KVHEADS = 8
HEAD = 128
ROTATED = (QHEADS + KVHEADS) * HEAD

HALF_PI = (1.5703125, 4.837512969970703e-4, 7.549789948768648e-8)
ROW = ("yh", "x")
COL = ("yl", "z4", "z2", "z1", "c")
SWAP = ((0, 1), (1, 0))
STEP = 256
WIDE = 512


def scaled_freq(within):
    base = jnp.exp(-(2.0 * within.astype(jnp.float32) / HEAD) * math.log(500000.0))
    wave = 2.0 * math.pi / base
    smooth = (8192.0 / wave - 1.0) / 3.0
    middle = (1.0 - smooth) * base / 8.0 + smooth * base
    return jnp.where(wave < 2048.0, base, jnp.where(wave > 8192.0, base / 8.0, middle))


def sine_cosine(angle):
    turns = jnp.floor(angle * (2.0 / math.pi) + 0.5)
    rest = angle
    for part in HALF_PI:
        rest = rest - turns * part
    square = rest * rest
    sine = rest + rest * square * (
        -1.6666654611e-1 + square * (8.3321608736e-3 + square * -1.9515295891e-4)
    )
    cosine = (
        1.0
        - 0.5 * square
        + square * square * (4.166664568298827e-2 + square * (-1.388731625493765e-3 + square * 2.443315711809948e-5))
    )
    quarter = turns.astype(jnp.int32)
    odd = (quarter & 1) == 1
    sine, cosine = jnp.where(odd, cosine, sine), jnp.where(odd, sine, cosine)
    sine = jnp.where((quarter & 2) == 2, -sine, sine)
    cosine = jnp.where(((quarter + 1) & 2) == 2, -cosine, cosine)
    return sine, cosine


def unrotate_kernel(positions_ref, grad_ref, out_ref):
    rows, width = grad_ref.shape
    col_start = lax.axis_index(COL) * width
    row = lax.broadcasted_iota(jnp.int32, (rows, rows), 0)
    column = lax.broadcasted_iota(jnp.int32, (rows, rows), 1)
    spread = jnp.where(row == column, positions_ref[...].astype(jnp.float32), 0.0)
    positions = jnp.sum(spread, axis=1, keepdims=True)
    lane = lax.broadcasted_iota(jnp.int32, (8, HEAD), 1)
    freq = scaled_freq(((col_start + lane) & (HEAD - 1)) >> 1)[:1]
    sine, cosine = sine_cosine(positions * freq)
    source = lax.broadcasted_iota(jnp.int32, (HEAD, HEAD), 0)
    target = lax.broadcasted_iota(jnp.int32, (HEAD, HEAD), 1)
    partner = jnp.where(source == (target ^ 1), jnp.where((target & 1) == 0, 1.0, -1.0), 0.0).astype(jnp.bfloat16)
    half = out_ref.shape[2]
    for start in range(0, width, HEAD):
        size = min(HEAD, width - start)
        block = grad_ref[:, start : start + size]
        swapped = jnp.dot(block, partner[:size, :size], preferred_element_type=jnp.float32)
        turned = block.astype(jnp.float32) * cosine[:, :size] + swapped * sine[:, :size]
        columns = col_start + start + lax.broadcasted_iota(jnp.int32, (rows, size), 1)
        result = jnp.where(columns < ROTATED, turned, block.astype(jnp.float32)).astype(jnp.bfloat16)
        for copy in range(out_ref.shape[0]):
            for core in range(out_ref.shape[1]):
                out_ref[copy, core, :, start : start + size] = result[core * half : (core + 1) * half]


def unrotate(grad, positions, copies, cores):
    rows, width = grad.shape
    return pl.pallas_call(
        unrotate_kernel,
        out_shape=jax.ShapeDtypeStruct((copies, cores, rows // cores, width), jnp.bfloat16),
        in_specs=[pl.BlockSpec(memory_space=pltpu.VMEM)] * 2,
        out_specs=pl.BlockSpec(memory_space=pltpu.VMEM),
        name="unrotate",
    )(positions.reshape(1, rows), grad)


def arrange_kernel(arrived_ref, out_ref, parts_ref, laid_ref, sem, out_sems):
    load = pltpu.make_async_copy(arrived_ref, parts_ref, sem)
    load.start()
    load.wait()
    width = parts_ref.shape[3]
    main = width // HEAD * HEAD
    rest = width - main
    yl, core = lax.axis_index("yl"), lax.axis_index("c")
    for far in range(2):
        for z4 in range(2):
            yh = (yl ^ far) * 2 + z4
            own = parts_ref[yh, core]
            other = parts_ref[yh, 1 - core]
            laid_ref[far, z4, :, :main] = own[:, :main]
            laid_ref[far, z4, :, main : 2 * main] = other[:, :main]
            laid_ref[far, z4, :, 2 * main : 2 * main + rest] = own[:, main:]
            laid_ref[far, z4, :, 2 * main + rest :] = other[:, main:]
    copies = [pltpu.make_async_copy(laid_ref, out_ref.at[i], out_sems.at[i]) for i in range(out_ref.shape[0])]
    for copy in copies:
        copy.start()
    for copy in copies:
        copy.wait()


def arrange(parts, copies):
    tokens, width = parts.shape[2:]
    return pl.pallas_call(
        arrange_kernel,
        out_shape=jax.ShapeDtypeStruct((copies, 2, 2, tokens, 2 * width), jnp.bfloat16),
        in_specs=[pl.BlockSpec(memory_space=pl.ANY)],
        out_specs=pl.BlockSpec(memory_space=pltpu.HBM),
        scratch_shapes=[
            pltpu.VMEM(parts.shape, parts.dtype),
            pltpu.VMEM((2, 2, tokens, 2 * width), parts.dtype),
            pltpu.SemaphoreType.DMA,
            pltpu.SemaphoreType.DMA((copies,)),
        ],
        compiler_params=pltpu.CompilerParams(vmem_limit_bytes=8 << 20),
        name="arrange",
    )(parts)


def total_of(grads_ref, own_ref, other_ref):
    groups, rows, width = grads_ref.shape
    main = own_ref.shape[0] // HEAD * HEAD
    last = jnp.concatenate([own_ref[main:], other_ref[main:]], axis=0)
    grads = grads_ref[...].reshape(groups * rows, width)
    total = jnp.dot(grads[:, :main], own_ref[:main], preferred_element_type=jnp.float32)
    total += jnp.dot(grads[:, main : 2 * main], other_ref[:main], preferred_element_type=jnp.float32)
    return total + jnp.dot(grads[:, 2 * main :], last, preferred_element_type=jnp.float32)


def load_part(arrived_ref, far, held_ref, sem):
    load = pltpu.make_async_copy(arrived_ref.at[:, far], held_ref, sem)
    load.start()
    load.wait()


def far_product_kernel(arrived_ref, own_ref, other_ref, out_ref, grads_ref, sem):
    @pl.when(pl.program_id(0) == 0)
    def _():
        load_part(arrived_ref, 1, grads_ref, sem)

    out_ref[...] = total_of(grads_ref, own_ref, other_ref).astype(out_ref.dtype)


def near_product_kernel(arrived_ref, own_ref, other_ref, added_ref, out_ref, grads_ref, sem, held_ref, out_sems):
    step = pl.program_id(0)

    @pl.when(step == 0)
    def _():
        load_part(arrived_ref, 0, grads_ref, sem)

    total = total_of(grads_ref, own_ref, other_ref) + added_ref[...].astype(jnp.float32)
    held_ref[step] = total.astype(held_ref.dtype)

    def store(at):
        return pltpu.make_async_copy(held_ref.at[at], out_ref.at[:, pl.ds(at * STEP, STEP)], out_sems.at[at])

    store(step).start()

    @pl.when(step == pl.num_programs(0) - 1)
    def _():
        for at in range(held_ref.shape[0]):
            store(at).wait()


def input_product(grads, own_weight, other_weight, added=None):
    groups, _, rows, width = grads.shape
    columns, model = own_weight.shape
    by_column = lambda step: (0, step)
    weights = [pl.BlockSpec((columns, STEP), by_column)] * 2
    part = [pl.BlockSpec((groups * rows, STEP), by_column)]
    near = added is not None
    steps = model // STEP
    store = [pltpu.VMEM((steps, groups * rows, STEP), jnp.bfloat16), pltpu.SemaphoreType.DMA((steps,))]
    return pl.pallas_call(
        near_product_kernel if near else far_product_kernel,
        grid=(model // STEP,),
        out_shape=jax.ShapeDtypeStruct((groups * rows, model), jnp.bfloat16),
        in_specs=[pl.BlockSpec(memory_space=pl.ANY)] + weights + part * near,
        out_specs=pl.BlockSpec(memory_space=pltpu.HBM) if near else part[0],
        scratch_shapes=[pltpu.VMEM((groups, rows, width), grads.dtype), pltpu.SemaphoreType.DMA] + store * near,
        compiler_params=pltpu.CompilerParams(vmem_limit_bytes=12 << 20),
        cost_estimate=pl.CostEstimate(flops=2 * groups * rows * width * model, bytes_accessed=4 << 20, transcendentals=0),
        name="near_product" if near else "far_product",
    )(grads, own_weight, other_weight, *([added] * near))


def blocks_of(groups, size):
    z1, z2, z4 = lax.axis_index("z1"), lax.axis_index("z2"), lax.axis_index("z4")
    for index in range(4 * groups):
        group = ((index >> 2 & 1) ^ z2) * 2 + ((index >> 3) ^ z1)
        place = pl.ds(pl.multiple_of(((index >> 1 & 1) ^ z4) * size, size), size)
        yield index * size, group, index & 1, place


def weight_product_kernel(side, arrived_ref, first_ref, second_ref, *refs):
    grads_ref, held_ref, turned_ref, sem = refs[-4:]
    groups, _, rows, width = grads_ref.shape
    columns = width // 2
    main = columns // HEAD * HEAD
    rest = columns - main
    half = rows // 2
    split = first_ref.shape[0]
    step = pl.program_id(0)
    early = step < pl.num_programs(0) // 2

    @pl.when(step == 0)
    def _():
        load = pltpu.make_async_copy(arrived_ref, grads_ref, sem)
        load.start()
        load.wait()
        for start, group, far, place in blocks_of(groups, half):
            held_ref[start : start + half, :main] = grads_ref[group, far, place, side * main : (side + 1) * main]
            last = 2 * main + side * rest
            held_ref[start : start + half, main:columns] = grads_ref[group, far, place, last : last + rest]
        held_ref[:, columns:] = jnp.zeros_like(held_ref[:, columns:])
        turned_ref[...] = held_ref[...].T

    total = jnp.dot(turned_ref[:columns, :split], first_ref[...], preferred_element_type=jnp.float32)
    total += jnp.dot(turned_ref[:columns, split:], second_ref[...], preferred_element_type=jnp.float32)
    if side == 0:
        left_ref, right_ref, out_ref = refs[:3]
        out_ref[...] = total + jnp.where(early, left_ref[...], right_ref[...]).astype(jnp.float32)
    else:
        left_ref, right_ref = refs[:2]

        @pl.when(early)
        def _():
            left_ref[...] = total.astype(left_ref.dtype)

        @pl.when(jnp.logical_not(early))
        def _():
            right_ref[...] = total.astype(right_ref.dtype)


def weight_product(grads, first, second, added=None):
    width = grads.shape[3]
    columns, (tokens, model) = width // 2, first.shape
    padded = pl.cdiv(columns, HEAD) * HEAD
    steps = model // WIDE
    by_column = lambda step: (0, step)
    whole = pl.BlockSpec((columns, WIDE), by_column)
    left = pl.BlockSpec((columns, WIDE), lambda step: (0, jnp.minimum(step, steps // 2 - 1)))
    right = pl.BlockSpec((columns, WIDE), lambda step: (0, jnp.maximum(step - steps // 2, 0)))
    own = added is not None
    return pl.pallas_call(
        functools.partial(weight_product_kernel, 0 if own else 1),
        grid=(steps,),
        out_shape=jax.ShapeDtypeStruct((columns, model), jnp.float32)
        if own
        else [jax.ShapeDtypeStruct((columns, model // 2), jnp.bfloat16)] * 2,
        in_specs=[pl.BlockSpec(memory_space=pl.ANY)]
        + [pl.BlockSpec((tokens, WIDE), by_column)] * 2
        + [left, right] * own,
        out_specs=whole if own else [left, right],
        scratch_shapes=[
            pltpu.VMEM(grads.shape, grads.dtype),
            pltpu.VMEM((2 * tokens, padded), jnp.bfloat16),
            pltpu.VMEM((padded, 2 * tokens), jnp.bfloat16),
            pltpu.SemaphoreType.DMA,
        ],
        compiler_params=pltpu.CompilerParams(vmem_limit_bytes=24 << 20),
        cost_estimate=pl.CostEstimate(flops=4 * tokens * columns * model, bytes_accessed=6 << 20, transcendentals=0),
        name="own_weight_product" if own else "other_weight_product",
    )(grads, first, second, *(added if own else ()))


def exchange(parts, axes):
    return lax.all_to_all(parts, axes, 0, 0, tiled=True)


def swapped(array, axis):
    return lax.ppermute(array, axis, SWAP)


def after(array, earlier):
    return lax.optimization_barrier((array, earlier))[0]


def doubled(array, axis):
    return jnp.concatenate([array, swapped(array, axis)], 0)


def per_device(inputs, weight, grad_out, positions):
    width = weight.shape[1]
    tokens, model = inputs.shape

    sent = unrotate(grad_out, positions, lax.axis_size("yh"), lax.axis_size("c"))
    own_weight = weight.T
    own_inputs = doubled(after(inputs, sent), "yl")
    arrived = exchange(sent.reshape(-1, tokens, width), ("yh", "c"))
    arrived = after(arrived, own_inputs)
    parts = arrange(arrived.reshape(sent.shape), lax.axis_size("x"))
    own_inputs = doubled(own_inputs, "z4")
    other_weight = swapped(after(own_weight, parts), "c")
    grads = exchange(parts, "x").reshape(-1, 2, 2 * tokens, 2 * width)
    own_inputs = doubled(own_inputs, "z2")

    far = input_product(grads, own_weight, other_weight)
    own_inputs = after(own_inputs, far)
    second = swapped(own_inputs, "z1")
    near = input_product(grads, own_weight, other_weight, swapped(far, "yl"))
    parts = exchange(near.reshape(-1, tokens, model), ("z2", "z1", "z4"))
    second = after(second, near)
    lent = [swapped(half, "c") for half in weight_product(grads, own_inputs, second)]
    weight_grad = weight_product(grads, own_inputs, second, lent).T
    parts, weight_grad = lax.optimization_barrier((parts, weight_grad))
    input_grad = parts.astype(jnp.float32).sum(axis=0).astype(jnp.bfloat16)
    return input_grad, weight_grad


def solution(mesh):
    sizes = {"yh": 4, "x": 4, "yl": 2, "z4": 2, "z2": 2, "z1": 2, "c": 2}
    finer = Mesh(mesh.devices.reshape(tuple(sizes.values())), tuple(sizes))
    in_specs = (P(COL, ROW), P(ROW, COL), P(ROW, COL), P(ROW))
    out_specs = (P(COL, ROW), P(ROW, COL))
    return jax.shard_map(per_device, mesh=finer, in_specs=in_specs, out_specs=out_specs, check_vma=False)
```
